32 devices in a mesh: rollout: 16 (over z, y, core), tensor: 2 (over x).
Axes of the slice: x: 2, y: 2, z: 4, core: 2. Of those that a mesh axis runs over, the one named last changes fastest.
Arguments:
- tokens: bfloat16 [4096, 8192], P('rollout', 'tensor'), may hold values from -6 to 6
- base_key_value_weight: bfloat16 [8192, 2, 1024], P(None, None, 'tensor'), may hold values from -0.0625 to 0.0625
- key_value_bias: bfloat16 [2, 1024], P(None, 'tensor'), may hold values from -3 to 3
- adapter_down_blocks: bfloat16 [8192, 2, 128], P('rollout'), may hold values from -0.0625 to 0.0625
- adapter_up_blocks: bfloat16 [2, 128, 1024], P(None, 'rollout', 'tensor'), may hold values from -0.29882812 to 0.29882812
- owner_shard_lookup: int32 [16], replicated, may hold values from 0 to 15, each once
- lengths: int32 [16, 8], P('rollout'), may hold values from 1 to 128, 256 in all within a row
- routes: int32 [4096], P('rollout'), may hold values from 0 to 15, as said below
Outputs:
- kv_cache: bfloat16 [8192, 2, 1024], P('rollout', None, 'tensor')
The draws below stay inside these ranges and needn't reach their ends.
Inputs may be any that keep to these rules, and one draw needn't show every extreme that they name: `owner_shard_lookup`: a permutation of the rollout indices. `routes`: the rows of one group name each destination at most 32 times; one destination, drawn from the seed, is named exactly 32 times by every group.
All inputs are finite; a program needn't handle non-finite values.
Results may differ from the reference program's by a relative error of at most 0.0048.
Values may be sent and summed in bfloat16 or wider, within the bound.
A program may use at most 128 MiB of HBM per device.

```python
import math
import jax
import jax.numpy as jnp
import numpy as np
from jax import lax

MODEL_FEATURES = 8192
HEAD = 128
UPDATE_RANK = 128
ROWS_SRC = 256
SEGS = 8
ROLLOUT_GROUPS = 16
KEY_VALUE_WIDTH = 1024
CAP = 32
SLOTS = 512
SEG_MOST = 128


def draw_routes(key, part):
    key = jax.random.fold_in(key, 11)
    hottest = jax.random.randint(jax.random.fold_in(key, 0), (), 0, ROLLOUT_GROUPS)

    def one_source(source):
        source_key = jax.random.fold_in(key, source + 1)
        pieces = []
        for index in range(CAP):
            pieces.append(jax.random.permutation(jax.random.fold_in(source_key, index), ROLLOUT_GROUPS - 1))
        offsets = jnp.concatenate(pieces)[:ROWS_SRC - CAP]
        others = (hottest + 1 + offsets) % ROLLOUT_GROUPS
        listed = jnp.concatenate([jnp.full((CAP,), hottest, jnp.int32), others.astype(jnp.int32)])
        shuffle = jax.random.permutation(jax.random.fold_in(source_key, CAP + 7), ROWS_SRC)
        return listed[shuffle]
    return jax.vmap(one_source)(jnp.arange(ROLLOUT_GROUPS)).reshape(-1).astype(jnp.int32)


def level_of(stream_key, shape, cuts, least, largest):
    level = 1.0
    for axis_at, blocks in cuts:
        steps = jax.random.uniform(jax.random.fold_in(jax.random.fold_in(stream_key, 6), axis_at), (blocks,), jnp.float32, least / len(cuts), largest / len(cuts))
        level = level * jnp.repeat(jnp.exp(steps), shape[axis_at] // blocks).reshape((-1,) + (1,) * (len(shape) - 1 - axis_at))
    return level


def split_up(amount, total, reach, skew):
    loads = [(1 << 20) // math.isqrt(standing ** skew) + 1 for standing in range(2, amount + 1)]
    surplus, given = total - reach - (amount - 1), [1] * (amount - 1)
    while surplus > 0:
        free = [i for i in range(amount - 1) if given[i] < reach]
        pool, budget = sum([loads[i] for i in free]), surplus
        for i in free:
            more = min(reach - given[i], max(1, budget * loads[i] // pool), surplus)
            given[i] = given[i] + more
            surplus = surplus - more
    return np.array([reach] + given)


def ragged_sizes(own_key, count, total, reach, slope):
    if count == 2:
        one = jax.random.randint(own_key, (), max(1, total - reach), min(reach, total - 1) + 1)
        return jnp.stack([one, total - one])
    sizes = jnp.asarray(split_up(count, total, reach, slope), jnp.int32)
    couples = (count - 1) // 2
    donor, taker = sizes[1:1 + 2 * couples:2], sizes[2:2 + 2 * couples:2]
    margin = jnp.minimum(donor - 1, reach - taker)
    shifted = jax.random.randint(jax.random.fold_in(own_key, 1), (couples,), 0, 1 << 20) % (margin + 1)
    sizes = sizes.at[1:1 + 2 * couples:2].set(donor - shifted).at[2:2 + 2 * couples:2].set(taker + shifted)
    return sizes[jax.random.permutation(jax.random.fold_in(own_key, 2), count)]


def normal_values(own_key, shape, deviation, limit, cuts=(), kind=jnp.bfloat16):
    array = jax.random.normal(own_key, shape, jnp.float32) * deviation
    if len(cuts) > 0:
        array = level_of(own_key, shape, cuts, -0.22, 0.18) * array
    return jnp.clip(array, min=-limit, max=limit).astype(kind)


def setup_inputs(seed: int = 0) -> dict:
    key_list = jax.random.split(jax.random.key(seed), 9)
    tokens = normal_values(key_list[0], (ROLLOUT_GROUPS * ROWS_SRC, MODEL_FEATURES), 1.0, 6.0, ((0, 16), (1, 2)))
    base_key_value_weight = normal_values(key_list[1], (MODEL_FEATURES, 2, KEY_VALUE_WIDTH), MODEL_FEATURES ** -0.5, 0.0625, ((2, 2),))
    key_value_bias = normal_values(key_list[2], (2, KEY_VALUE_WIDTH), 0.5, 3.0, ((1, 2),))
    adapter_down_blocks = normal_values(key_list[3], (MODEL_FEATURES, 2, UPDATE_RANK), MODEL_FEATURES ** -0.5, 0.0625, ((0, 16),))
    adapter_up_blocks = normal_values(key_list[4], (2, UPDATE_RANK, KEY_VALUE_WIDTH), 0.05, 0.29882812, ((1, 16), (2, 2)))
    owner_shard_lookup = jax.random.permutation(key_list[5], ROLLOUT_GROUPS).astype(jnp.int32)
    lengths = jax.vmap(lambda own: ragged_sizes(own, SEGS, ROWS_SRC, SEG_MOST, 2))(jax.random.split(key_list[6], ROLLOUT_GROUPS)).reshape((ROLLOUT_GROUPS, SEGS)).astype(jnp.int32)
    routes = draw_routes(jax.random.fold_in(key_list[8], 71), 0)
    return dict(tokens=tokens, base_key_value_weight=base_key_value_weight, key_value_bias=key_value_bias, adapter_down_blocks=adapter_down_blocks, adapter_up_blocks=adapter_up_blocks, owner_shard_lookup=owner_shard_lookup, lengths=lengths, routes=routes)


adapter_scale = 2.0
rope_base = 1000000.0


def positions_of(lengths_row, row_count):
    ends = jnp.cumsum(lengths_row)
    starts = ends - lengths_row
    index = jnp.arange(row_count, dtype=jnp.int32)
    begins = jnp.max(jnp.where(starts[None, :] <= index[:, None], starts[None, :], 0), axis=1)
    return (index - begins).astype(jnp.int32)


def rotate(keys, places):
    half_width = HEAD // 2
    frequency = rope_base ** (-(jnp.arange(half_width, dtype=jnp.float32) * 2.0) / HEAD)
    angles = places.astype(jnp.float32)[:, None] * frequency[None, :]
    cosine = jnp.cos(angles)[:, None, :]
    sine = jnp.sin(angles)[:, None, :]
    shaped = keys.reshape(keys.shape[0], -1, HEAD)
    first = shaped[..., :half_width]
    second = shaped[..., half_width:]
    turned = jnp.concatenate([first * cosine - second * sine, second * cosine + first * sine], axis=-1)
    return turned.reshape(keys.shape)


def finish_rows(summed, places, key_value_bias):
    width = key_value_bias.shape[1]
    shaped = summed.reshape(summed.shape[0], 2, width) + key_value_bias.astype(jnp.float32)[None]
    keys = rotate(shaped[:, 0], places)
    return jnp.stack([keys, shaped[:, 1]], axis=1)


def reference(tokens, base_key_value_weight, key_value_bias, adapter_down_blocks, adapter_up_blocks, owner_shard_lookup, lengths, routes):
    inverse_permutation = jnp.zeros((ROLLOUT_GROUPS,), jnp.int32).at[owner_shard_lookup].set(jnp.arange(ROLLOUT_GROUPS, dtype=jnp.int32))
    down_factor = adapter_down_blocks.reshape(ROLLOUT_GROUPS, MODEL_FEATURES // ROLLOUT_GROUPS, 2, UPDATE_RANK)[inverse_permutation].reshape(MODEL_FEATURES, 2, UPDATE_RANK)
    up_factor = adapter_up_blocks.reshape(2, ROLLOUT_GROUPS, UPDATE_RANK // ROLLOUT_GROUPS, KEY_VALUE_WIDTH)[:, inverse_permutation].reshape(2, UPDATE_RANK, KEY_VALUE_WIDTH)
    weight_update = jnp.einsum("ohd,hde->ohe", down_factor.astype(jnp.float32), up_factor.astype(jnp.float32))
    merged_weight = (base_key_value_weight.astype(jnp.float32) + adapter_scale * weight_update).astype(jnp.bfloat16)
    merged_flat = merged_weight.reshape(MODEL_FEATURES, 2 * KEY_VALUE_WIDTH)
    places = jax.vmap(lambda row: positions_of(row, ROWS_SRC))(lengths)
    token_blocks = tokens.reshape(ROLLOUT_GROUPS, ROWS_SRC, MODEL_FEATURES)

    def project_group(inputs):
        block, block_places = inputs
        summed = jnp.dot(block, merged_flat, preferred_element_type=jnp.float32)
        return finish_rows(summed, block_places, key_value_bias).astype(jnp.bfloat16)

    cache_rows = lax.map(project_group, (token_blocks, places))
    target = routes.reshape(ROLLOUT_GROUPS, ROWS_SRC)
    matches = (target[:, :, None] == jnp.arange(ROLLOUT_GROUPS, dtype=jnp.int32)[None, None, :]).astype(jnp.int32)
    order_in = jnp.sum((jnp.cumsum(matches, axis=1) - matches) * matches, axis=2)
    sources = jnp.arange(ROLLOUT_GROUPS, dtype=jnp.int32)[:, None]
    slot = (target * SLOTS + sources * CAP + order_in).astype(jnp.int32)
    result = jnp.zeros((ROLLOUT_GROUPS * SLOTS, 2, KEY_VALUE_WIDTH), jnp.bfloat16)
    return result.at[slot.reshape(-1)].set(cache_rows.reshape(ROLLOUT_GROUPS * ROWS_SRC, 2, KEY_VALUE_WIDTH))
```

```python
import jax
import jax.numpy as jnp
from jax import lax
from jax.sharding import PartitionSpec as P

HEAD = 128


adapter_scale = 2.0
rope_base = 1000000.0


def positions_of(lengths_row, row_count):
    ends = jnp.cumsum(lengths_row)
    starts = ends - lengths_row
    index = jnp.arange(row_count, dtype=jnp.int32)
    begins = jnp.max(jnp.where(starts[None, :] <= index[:, None], starts[None, :], 0), axis=1)
    return index - begins


def rotate(keys, places):
    half_width = HEAD // 2
    frequency = rope_base ** (-(jnp.arange(half_width, dtype=jnp.float32) * 2.0) / HEAD)
    angles = places.astype(jnp.float32)[:, None] * frequency[None, :]
    cosine = jnp.cos(angles)[:, None, :]
    sine = jnp.sin(angles)[:, None, :]
    shaped = keys.reshape(keys.shape[0], -1, HEAD)
    first = shaped[..., :half_width]
    second = shaped[..., half_width:]
    turned = jnp.concatenate(
        [first * cosine - second * sine, second * cosine + first * sine], axis=-1
    )
    return turned.reshape(keys.shape)


def slot_index(target, group_count, capacity):
    matches = (target[:, None] == jnp.arange(group_count, dtype=jnp.int32)[None, :]).astype(
        jnp.int32
    )
    order_in = jnp.sum((jnp.cumsum(matches, axis=0) - matches) * matches, axis=1)
    return target * capacity + order_in


def body(
    tokens,
    base_key_value_weight,
    key_value_bias,
    adapter_down_blocks,
    adapter_up_blocks,
    owner_shard_lookup,
    lengths,
    routes,
):
    group_count = lax.axis_size("rollout")
    row_count = tokens.shape[0]
    capacity = 2 * row_count // group_count
    width = base_key_value_weight.shape[2]
    model_width = base_key_value_weight.shape[0]
    inverse_permutation = (
        jnp.zeros((group_count,), jnp.int32)
        .at[owner_shard_lookup]
        .set(jnp.arange(group_count, dtype=jnp.int32))
    )
    up_persisted = lax.all_gather(adapter_up_blocks, "rollout", axis=0, tiled=False)
    down_persisted = lax.all_gather(adapter_down_blocks, "rollout", axis=0, tiled=False)
    rows = lax.all_gather(tokens, "tensor", axis=1, tiled=True)
    down = down_persisted[inverse_permutation].reshape(model_width, -1)
    up = up_persisted[inverse_permutation].transpose(1, 0, 2, 3).reshape(2, -1, width)
    rank = up.shape[1]
    low = jnp.dot(rows, down, preferred_element_type=jnp.float32)
    low = (adapter_scale * low).astype(jnp.bfloat16).reshape(row_count, 2, rank)
    update = jnp.einsum("nsr,src->nsc", low, up, preferred_element_type=jnp.float32)
    summed = jnp.einsum(
        "nf,fsc->nsc", rows, base_key_value_weight, preferred_element_type=jnp.float32
    )
    shaped = summed + update + key_value_bias.astype(jnp.float32)[None]
    places = positions_of(lengths[0], row_count)
    keys = rotate(shaped[:, 0], places)
    finished = jnp.concatenate([keys, shaped[:, 1]], axis=1).astype(jnp.bfloat16)
    slot_count = group_count * capacity
    send_slots = slot_index(routes, group_count, capacity)
    selector = (jnp.arange(slot_count, dtype=jnp.int32)[:, None] == send_slots[None, :]).astype(
        jnp.bfloat16
    )
    outgoing = jnp.dot(selector, finished, preferred_element_type=jnp.float32).astype(jnp.bfloat16)
    arrived = lax.all_to_all(
        outgoing.reshape(group_count, capacity, 2 * width),
        "rollout",
        split_axis=0,
        concat_axis=0,
        tiled=True,
    )
    return arrived.reshape(slot_count, 2, width)


def solution(mesh):
    in_specs = (
        P("rollout", "tensor"),
        P(None, None, "tensor"),
        P(None, "tensor"),
        P("rollout", None, None),
        P(None, "rollout", "tensor"),
        P(),
        P("rollout", None),
        P("rollout"),
    )
    out_specs = P("rollout", None, "tensor")
    return jax.shard_map(body, mesh=mesh, in_specs=in_specs, out_specs=out_specs, check_vma=False)
```

```python
import functools

import jax
import jax.numpy as jnp
from jax import lax
from jax.experimental import pallas as pl
from jax.experimental.pallas import tpu as pltpu
from jax.sharding import PartitionSpec as P

HEAD = 128


adapter_scale = 2.0
rope_base = 1000000.0


def positions_of(lengths_row, row_count):
    ends = jnp.cumsum(lengths_row)
    starts = ends - lengths_row
    index = jnp.arange(row_count, dtype=jnp.int32)
    begins = jnp.max(jnp.where(starts[None, :] <= index[:, None], starts[None, :], 0), axis=1)
    return index - begins


def rotate(keys, places):
    half_width = HEAD // 2
    frequency = rope_base ** (-(jnp.arange(half_width, dtype=jnp.float32) * 2.0) / HEAD)
    angles = places.astype(jnp.float32)[:, None] * frequency[None, :]
    cosine = jnp.cos(angles)[:, None, :]
    sine = jnp.sin(angles)[:, None, :]
    shaped = keys.reshape(keys.shape[0], -1, HEAD)
    first = shaped[..., :half_width]
    second = shaped[..., half_width:]
    turned = jnp.concatenate(
        [first * cosine - second * sine, second * cosine + first * sine], axis=-1
    )
    return turned.reshape(keys.shape)


def slot_index(target, group_count, capacity):
    matches = (target[:, None] == jnp.arange(group_count, dtype=jnp.int32)[None, :]).astype(
        jnp.int32
    )
    order_in = jnp.sum((jnp.cumsum(matches, axis=0) - matches) * matches, axis=1)
    return target * capacity + order_in


def gather_kernel(
    groups,
    shards,
    tokens,
    factors,
    rows_out,
    factors_out,
    local_sem,
    token_send,
    token_recv,
    factor_send,
    factor_recv,
    forward_send,
    forward_recv,
):
    me = lax.axis_index("rollout")
    part = lax.axis_index("tensor")
    chips = groups // 2
    chip, core = me // 2, me % 2
    sibling = chip * 2 + (1 - core)
    features = tokens.shape[1]

    def same_core(step):
        return ((chip + step + chips) % chips) * 2 + core

    barrier = pltpu.get_barrier_semaphore()
    for step in range(1, shards):
        pl.semaphore_signal(barrier, inc=1, device_id={"tensor": (part + step) % shards})
    for step in range(1, chips):
        pl.semaphore_signal(barrier, inc=1, device_id={"rollout": same_core(step)})
    pl.semaphore_signal(barrier, inc=1, device_id={"rollout": sibling})
    pl.semaphore_wait(barrier, shards - 1 + chips - 1 + 1)

    columns = pl.ds(pl.multiple_of(part * features, features), features)
    copies = []
    for step in range(1, shards):
        copies.append(
            pltpu.make_async_remote_copy(
                src_ref=tokens,
                dst_ref=rows_out.at[:, columns],
                send_sem=token_send.at[step],
                recv_sem=token_recv.at[step],
                device_id={"tensor": (part + step) % shards},
            )
        )
        copies[-1].start()
    sends = []
    for step in range(1, chips):
        sends.append(
            pltpu.make_async_remote_copy(
                src_ref=factors,
                dst_ref=factors_out.at[me],
                send_sem=factor_send.at[step],
                recv_sem=factor_recv.at[step],
                device_id={"rollout": same_core(step)},
            )
        )
        sends[-1].start()
    copies.append(
        pltpu.make_async_remote_copy(
            src_ref=factors,
            dst_ref=factors_out.at[me],
            send_sem=forward_send.at[0],
            recv_sem=forward_recv.at[0],
            device_id={"rollout": sibling},
        )
    )
    copies[-1].start()
    own_rows = pltpu.make_async_copy(tokens, rows_out.at[:, columns], local_sem.at[0])
    own_rows.start()
    own_factors = pltpu.make_async_copy(factors, factors_out.at[me], local_sem.at[1])
    own_factors.start()
    for step in range(1, chips):
        sends[step - 1].wait_recv()
        source = same_core(-step)
        copies.append(
            pltpu.make_async_remote_copy(
                src_ref=factors_out.at[source],
                dst_ref=factors_out.at[source],
                send_sem=forward_send.at[step],
                recv_sem=forward_recv.at[step],
                device_id={"rollout": sibling},
            )
        )
        copies[-1].start()
    for copy in sends:
        copy.wait_send()
    for copy in copies:
        copy.wait()
    own_rows.wait()
    own_factors.wait()


def gather_all(tokens, factors, groups, shards):
    chips = groups // 2
    rows, features = tokens.shape
    dma = pltpu.SemaphoreType.DMA
    return pl.pallas_call(
        functools.partial(gather_kernel, groups, shards),
        out_shape=(
            jax.ShapeDtypeStruct((rows, shards * features), tokens.dtype),
            jax.ShapeDtypeStruct((groups,) + factors.shape, factors.dtype),
        ),
        in_specs=[pl.BlockSpec(memory_space=pl.ANY)] * 2,
        out_specs=[pl.BlockSpec(memory_space=pl.ANY)] * 2,
        scratch_shapes=[
            dma((2,)),
            dma((shards,)),
            dma((shards,)),
            dma((chips,)),
            dma((chips,)),
            dma((chips,)),
            dma((chips,)),
        ],
        compiler_params=pltpu.CompilerParams(collective_id=0, has_side_effects=True),
    )(tokens, factors)


def exchange_kernel(groups, outgoing, arrived, local_sem, send_sem, recv_sem):
    me = lax.axis_index("rollout")
    barrier = pltpu.get_barrier_semaphore()
    for step in range(1, groups):
        pl.semaphore_signal(barrier, inc=1, device_id={"rollout": (me + step) % groups})
    pl.semaphore_wait(barrier, groups - 1)
    copies = []
    for step in range(1, groups):
        peer = (me + step) % groups
        copies.append(
            pltpu.make_async_remote_copy(
                src_ref=outgoing.at[peer],
                dst_ref=arrived.at[me],
                send_sem=send_sem.at[step],
                recv_sem=recv_sem.at[step],
                device_id={"rollout": peer},
            )
        )
        copies[-1].start()
    own = pltpu.make_async_copy(outgoing.at[me], arrived.at[me], local_sem)
    own.start()
    for copy in copies:
        copy.wait()
    own.wait()


def exchange(outgoing, groups):
    dma = pltpu.SemaphoreType.DMA
    return pl.pallas_call(
        functools.partial(exchange_kernel, groups),
        out_shape=jax.ShapeDtypeStruct(outgoing.shape, outgoing.dtype),
        in_specs=[pl.BlockSpec(memory_space=pl.ANY)],
        out_specs=pl.BlockSpec(memory_space=pl.ANY),
        scratch_shapes=[dma, dma((groups,)), dma((groups,))],
        compiler_params=pltpu.CompilerParams(collective_id=1, has_side_effects=True),
    )(outgoing)


def low_kernel(lookup, rows, down, low, total):
    step = pl.program_id(0)

    @pl.when(step == 0)
    def _():
        total[...] = jnp.zeros_like(total)

    total[...] += jnp.dot(rows[...], down[0], preferred_element_type=jnp.float32)

    @pl.when(step == pl.num_programs(0) - 1)
    def _():
        low[...] = (adapter_scale * total[...]).astype(low.dtype)


def low_rank(lookup, rows, factors, block_rows):
    row_count = rows.shape[0]
    groups, _, columns = factors.shape
    return pl.pallas_call(
        low_kernel,
        out_shape=jax.ShapeDtypeStruct((row_count, columns), jnp.bfloat16),
        grid_spec=pltpu.PrefetchScalarGridSpec(
            num_scalar_prefetch=1,
            grid=(groups,),
            in_specs=[
                pl.BlockSpec((row_count, block_rows), lambda i, lookup: (0, lookup[i])),
                pl.BlockSpec((1, block_rows, columns), lambda i, lookup: (i, 0, 0)),
            ],
            out_specs=pl.BlockSpec((row_count, columns), lambda i, lookup: (0, 0)),
            scratch_shapes=[pltpu.VMEM((row_count, columns), jnp.float32)],
        ),
    )(lookup, rows, factors)


def body(
    tokens,
    base_key_value_weight,
    key_value_bias,
    adapter_down_blocks,
    adapter_up_blocks,
    owner_shard_lookup,
    lengths,
    routes,
):
    group_count = lax.axis_size("rollout")
    row_count = tokens.shape[0]
    capacity = 2 * row_count // group_count
    width = base_key_value_weight.shape[2]
    inverse_permutation = (
        jnp.zeros((group_count,), jnp.int32)
        .at[owner_shard_lookup]
        .set(jnp.arange(group_count, dtype=jnp.int32))
    )
    block_rows = adapter_down_blocks.shape[0]
    low_width = 2 * adapter_down_blocks.shape[2]
    factors = jnp.concatenate(
        [
            adapter_down_blocks.reshape(block_rows, low_width),
            adapter_up_blocks.reshape(-1, low_width),
        ],
        axis=0,
    )
    rows, all_factors = gather_all(tokens, factors, group_count, lax.axis_size("tensor"))
    low = low_rank(owner_shard_lookup, rows, all_factors, block_rows)
    low = low.reshape(row_count, 2, -1)
    up_blocks = all_factors[:, block_rows:].reshape((group_count,) + adapter_up_blocks.shape)
    up = up_blocks[inverse_permutation].transpose(1, 0, 2, 3).reshape(2, -1, width)
    update = jnp.einsum("nsr,src->nsc", low, up, preferred_element_type=jnp.float32)
    summed = jnp.einsum(
        "nf,fsc->nsc", rows, base_key_value_weight, preferred_element_type=jnp.float32
    )
    shaped = summed + update + key_value_bias.astype(jnp.float32)[None]
    places = positions_of(lengths[0], row_count)
    keys = rotate(shaped[:, 0], places)
    finished = jnp.concatenate([keys, shaped[:, 1]], axis=1).astype(jnp.bfloat16)
    slot_count = group_count * capacity
    send_slots = slot_index(routes, group_count, capacity)
    selector = (jnp.arange(slot_count, dtype=jnp.int32)[:, None] == send_slots[None, :]).astype(
        jnp.bfloat16
    )
    outgoing = jnp.dot(selector, finished, preferred_element_type=jnp.float32).astype(jnp.bfloat16)
    arrived = exchange(outgoing.reshape(group_count, capacity, 2 * width), group_count)
    return arrived.reshape(slot_count, 2, width)


def solution(mesh):
    in_specs = (
        P("rollout", "tensor"),
        P(None, None, "tensor"),
        P(None, "tensor"),
        P("rollout", None, None),
        P(None, "rollout", "tensor"),
        P(),
        P("rollout", None),
        P("rollout"),
    )
    out_specs = P("rollout", None, "tensor")
    return jax.shard_map(body, mesh=mesh, in_specs=in_specs, out_specs=out_specs, check_vma=False)
```

```python
import functools

import jax
import jax.numpy as jnp
from jax import lax
from jax.experimental import pallas as pl
from jax.experimental.pallas import tpu as pltpu
from jax.sharding import PartitionSpec as P

HEAD = 128


adapter_scale = 2.0
rope_base = 1000000.0


def positions_of(lengths_row, row_count):
    ends = jnp.cumsum(lengths_row)
    starts = ends - lengths_row
    index = jnp.arange(row_count, dtype=jnp.int32)
    begins = jnp.max(jnp.where(starts[None, :] <= index[:, None], starts[None, :], 0), axis=1)
    return index - begins


def rotate(keys, places):
    half_width = HEAD // 2
    frequency = rope_base ** (-(jnp.arange(half_width, dtype=jnp.float32) * 2.0) / HEAD)
    angles = places.astype(jnp.float32)[:, None] * frequency[None, :]
    cosine = jnp.cos(angles)[:, None, :]
    sine = jnp.sin(angles)[:, None, :]
    shaped = keys.reshape(keys.shape[0], -1, HEAD)
    first = shaped[..., :half_width]
    second = shaped[..., half_width:]
    turned = jnp.concatenate(
        [first * cosine - second * sine, second * cosine + first * sine], axis=-1
    )
    return turned.reshape(keys.shape)


def slot_index(target, group_count, capacity):
    matches = (target[:, None] == jnp.arange(group_count, dtype=jnp.int32)[None, :]).astype(
        jnp.int32
    )
    order_in = jnp.sum((jnp.cumsum(matches, axis=0) - matches) * matches, axis=1)
    return target * capacity + order_in


CHUNKS = 4


def gather_kernel(
    groups,
    shards,
    inverse,
    tokens,
    down,
    up,
    rows_out,
    low_out,
    up_out,
    down_all,
    local_sem,
    token_send,
    token_recv,
    down_send,
    down_recv,
    up_send,
    up_recv,
    forward_send,
    forward_recv,
    low_send,
    low_recv,
):
    me = lax.axis_index("rollout")
    part = lax.axis_index("tensor")
    chips = groups // 2
    chip, core = me // 2, me % 2
    sibling = chip * 2 + (1 - core)
    row_count, features = tokens.shape
    block_rows = down.shape[0]

    def same_core(step):
        return ((chip + step + chips) % chips) * 2 + core

    barrier = pltpu.get_barrier_semaphore()
    for step in range(1, shards):
        pl.semaphore_signal(barrier, inc=1, device_id={"tensor": (part + step) % shards})
    for step in range(1, groups):
        pl.semaphore_signal(barrier, inc=1, device_id={"rollout": (me + step) % groups})
    pl.semaphore_wait(barrier, shards - 1 + groups - 1)

    columns = pl.ds(pl.multiple_of(part * features, features), features)
    chunk_rows = row_count // CHUNKS
    copies = []
    sends = []
    for step in range(1, chips):
        sends.append(
            pltpu.make_async_remote_copy(
                src_ref=down,
                dst_ref=down_all.at[me],
                send_sem=down_send.at[step],
                recv_sem=down_recv.at[step],
                device_id={"rollout": same_core(step)},
            )
        )
        sends[-1].start()
    for chunk in range(CHUNKS):
        for step in range(1, shards):
            piece = pl.ds(chunk * chunk_rows, chunk_rows)
            copies.append(
                pltpu.make_async_remote_copy(
                    src_ref=tokens.at[piece],
                    dst_ref=rows_out.at[piece, columns],
                    send_sem=token_send.at[step, chunk],
                    recv_sem=token_recv.at[step, chunk],
                    device_id={"tensor": (part + step) % shards},
                )
            )
            copies[-1].start()
    copies.append(
        pltpu.make_async_remote_copy(
            src_ref=down,
            dst_ref=down_all.at[me],
            send_sem=forward_send.at[0],
            recv_sem=forward_recv.at[0],
            device_id={"rollout": sibling},
        )
    )
    copies[-1].start()
    for step in range(1, groups):
        copies.append(
            pltpu.make_async_remote_copy(
                src_ref=up,
                dst_ref=up_out.at[me],
                send_sem=up_send.at[step],
                recv_sem=up_recv.at[step],
                device_id={"rollout": (me + step) % groups},
            )
        )
        copies[-1].start()
    own = [
        pltpu.make_async_copy(tokens, rows_out.at[:, columns], local_sem.at[0]),
        pltpu.make_async_copy(down, down_all.at[me], local_sem.at[1]),
        pltpu.make_async_copy(up, up_out.at[me], local_sem.at[2]),
    ]
    for copy in own:
        copy.start()
    for step in range(1, chips):
        sends[step - 1].wait_recv()
        source = same_core(-step)
        copies.append(
            pltpu.make_async_remote_copy(
                src_ref=down_all.at[source],
                dst_ref=down_all.at[source],
                send_sem=forward_send.at[step],
                recv_sem=forward_recv.at[step],
                device_id={"rollout": sibling},
            )
        )
        copies[-1].start()
    for copy in sends:
        copy.wait_send()
    for copy in copies:
        copy.wait()
    for copy in own:
        copy.wait()

    total = jnp.zeros(low_out.shape[1:], jnp.float32)
    for owner in range(groups):
        block = pl.ds(owner * block_rows, block_rows)
        factor = down_all[inverse[owner]]
        total += jnp.dot(rows_out[:, block], factor, preferred_element_type=jnp.float32)
    low_out[part] = (adapter_scale * total).astype(low_out.dtype)
    copies = []
    for step in range(1, shards):
        copies.append(
            pltpu.make_async_remote_copy(
                src_ref=low_out.at[part],
                dst_ref=low_out.at[part],
                send_sem=low_send.at[step],
                recv_sem=low_recv.at[step],
                device_id={"tensor": (part + step) % shards},
            )
        )
        copies[-1].start()
    for copy in copies:
        copy.wait()


def gather_all(inverse, tokens, down, up, groups, shards):
    chips = groups // 2
    rows, features = tokens.shape
    dma = pltpu.SemaphoreType.DMA
    vmem = pl.BlockSpec(memory_space=pltpu.VMEM)
    hbm = pl.BlockSpec(memory_space=pl.ANY)
    return pl.pallas_call(
        functools.partial(gather_kernel, groups, shards),
        out_shape=(
            jax.ShapeDtypeStruct((rows, shards * features), tokens.dtype),
            jax.ShapeDtypeStruct((shards, rows, down.shape[1]), jnp.bfloat16),
            jax.ShapeDtypeStruct((groups,) + up.shape, up.dtype),
        ),
        in_specs=[pl.BlockSpec(memory_space=pltpu.SMEM), hbm, vmem, vmem],
        out_specs=[vmem, vmem, vmem],
        scratch_shapes=[
            pltpu.VMEM((groups,) + down.shape, down.dtype),
            dma((3,)),
            dma((shards, CHUNKS)),
            dma((shards, CHUNKS)),
            dma((chips,)),
            dma((chips,)),
            dma((groups,)),
            dma((groups,)),
            dma((chips,)),
            dma((chips,)),
            dma((shards,)),
            dma((shards,)),
        ],
        compiler_params=pltpu.CompilerParams(
            collective_id=0, has_side_effects=True, vmem_limit_bytes=24 * 1024 * 1024
        ),
    )(inverse, tokens, down, up)


def exchange_kernel(groups, outgoing, arrived, local_sem, send_sem, recv_sem):
    me = lax.axis_index("rollout")
    barrier = pltpu.get_barrier_semaphore()
    for step in range(1, groups):
        pl.semaphore_signal(barrier, inc=1, device_id={"rollout": (me + step) % groups})
    pl.semaphore_wait(barrier, groups - 1)
    copies = []
    for step in range(1, groups):
        peer = (me + step) % groups
        copies.append(
            pltpu.make_async_remote_copy(
                src_ref=outgoing.at[peer],
                dst_ref=arrived.at[me],
                send_sem=send_sem.at[step],
                recv_sem=recv_sem.at[step],
                device_id={"rollout": peer},
            )
        )
        copies[-1].start()
    own = pltpu.make_async_copy(outgoing.at[me], arrived.at[me], local_sem)
    own.start()
    for copy in copies:
        copy.wait()
    own.wait()


def exchange(outgoing, groups):
    dma = pltpu.SemaphoreType.DMA
    return pl.pallas_call(
        functools.partial(exchange_kernel, groups),
        out_shape=jax.ShapeDtypeStruct(outgoing.shape, outgoing.dtype),
        in_specs=[pl.BlockSpec(memory_space=pl.ANY)],
        out_specs=pl.BlockSpec(memory_space=pl.ANY),
        scratch_shapes=[dma, dma((groups,)), dma((groups,))],
        compiler_params=pltpu.CompilerParams(collective_id=1, has_side_effects=True),
    )(outgoing)


def body(
    tokens,
    base_key_value_weight,
    key_value_bias,
    adapter_down_blocks,
    adapter_up_blocks,
    owner_shard_lookup,
    lengths,
    routes,
):
    group_count = lax.axis_size("rollout")
    row_count = tokens.shape[0]
    capacity = 2 * row_count // group_count
    width = base_key_value_weight.shape[2]
    order = jnp.arange(group_count, dtype=jnp.int32)
    inverse_permutation = jnp.sum(
        jnp.where(owner_shard_lookup[None, :] == order[:, None], order[None, :], 0), axis=1
    )
    block_rows = adapter_down_blocks.shape[0]
    shards = lax.axis_size("tensor")
    low_width = 2 * adapter_down_blocks.shape[2]
    down_part = lax.dynamic_slice_in_dim(
        adapter_down_blocks.reshape(block_rows, low_width),
        lax.axis_index("tensor") * (low_width // shards),
        low_width // shards,
        axis=1,
    )
    rows, low, up_blocks = gather_all(
        inverse_permutation,
        tokens,
        down_part,
        adapter_up_blocks.reshape(-1, width),
        group_count,
        shards,
    )
    low = low.transpose(1, 0, 2).reshape(row_count, 2, -1)
    up_blocks = up_blocks.reshape((group_count,) + adapter_up_blocks.shape)
    up = up_blocks[inverse_permutation].transpose(1, 0, 2, 3).reshape(2, -1, width)
    update = jnp.einsum("nsr,src->nsc", low, up, preferred_element_type=jnp.float32)
    summed = jnp.einsum(
        "nf,fsc->nsc", rows, base_key_value_weight, preferred_element_type=jnp.float32
    )
    shaped = summed + update + key_value_bias.astype(jnp.float32)[None]
    places = positions_of(lengths[0], row_count)
    keys = rotate(shaped[:, 0], places)
    finished = jnp.concatenate([keys, shaped[:, 1]], axis=1).astype(jnp.bfloat16)
    slot_count = group_count * capacity
    send_slots = slot_index(routes, group_count, capacity)
    selector = (jnp.arange(slot_count, dtype=jnp.int32)[:, None] == send_slots[None, :]).astype(
        jnp.bfloat16
    )
    outgoing = jnp.dot(selector, finished, preferred_element_type=jnp.float32).astype(jnp.bfloat16)
    arrived = exchange(outgoing.reshape(group_count, capacity, 2 * width), group_count)
    return arrived.reshape(slot_count, 2, width)


def solution(mesh):
    in_specs = (
        P("rollout", "tensor"),
        P(None, None, "tensor"),
        P(None, "tensor"),
        P("rollout", None, None),
        P(None, "rollout", "tensor"),
        P(),
        P("rollout", None),
        P("rollout"),
    )
    out_specs = P("rollout", None, "tensor")
    return jax.shard_map(body, mesh=mesh, in_specs=in_specs, out_specs=out_specs, check_vma=False)
```

```python
import functools

import jax
import jax.numpy as jnp
from jax import lax
from jax.experimental import pallas as pl
from jax.experimental.pallas import tpu as pltpu
from jax.sharding import PartitionSpec as P

HEAD = 128


adapter_scale = 2.0
rope_base = 1000000.0


def positions_of(lengths_row, row_count):
    ends = jnp.cumsum(lengths_row)
    starts = ends - lengths_row
    index = jnp.arange(row_count, dtype=jnp.int32)
    begins = jnp.max(jnp.where(starts[None, :] <= index[:, None], starts[None, :], 0), axis=1)
    return index - begins


def rotate(keys, places):
    half_width = HEAD // 2
    frequency = rope_base ** (-(jnp.arange(half_width, dtype=jnp.float32) * 2.0) / HEAD)
    angles = places.astype(jnp.float32)[:, None] * frequency[None, :]
    cosine = jnp.cos(angles)[:, None, :]
    sine = jnp.sin(angles)[:, None, :]
    shaped = keys.reshape(keys.shape[0], -1, HEAD)
    first = shaped[..., :half_width]
    second = shaped[..., half_width:]
    turned = jnp.concatenate(
        [first * cosine - second * sine, second * cosine + first * sine], axis=-1
    )
    return turned.reshape(keys.shape)


def slot_index(target, group_count, capacity):
    matches = (target[:, None] == jnp.arange(group_count, dtype=jnp.int32)[None, :]).astype(
        jnp.int32
    )
    order_in = jnp.sum((jnp.cumsum(matches, axis=0) - matches) * matches, axis=1)
    return target * capacity + order_in


CHUNKS = 4


def gather_kernel(
    groups,
    shards,
    inverse,
    tokens,
    down,
    up,
    rows_out,
    low_out,
    up_out,
    down_all,
    local_sem,
    token_send,
    token_recv,
    down_send,
    down_recv,
    up_send,
    up_recv,
    forward_send,
    forward_recv,
    low_send,
    low_recv,
):
    me = lax.axis_index("rollout")
    part = lax.axis_index("tensor")
    chips = groups // 2
    chip, core = me // 2, me % 2
    sibling = chip * 2 + (1 - core)
    row_count, features = tokens.shape
    block_rows = down.shape[0]

    def same_core(step):
        return ((chip + step + chips) % chips) * 2 + core

    barrier = pltpu.get_barrier_semaphore()
    for step in range(1, shards):
        pl.semaphore_signal(barrier, inc=1, device_id={"tensor": (part + step) % shards})
    for step in range(1, groups):
        pl.semaphore_signal(barrier, inc=1, device_id={"rollout": (me + step) % groups})
    pl.semaphore_wait(barrier, shards - 1 + groups - 1)

    columns = pl.ds(pl.multiple_of(part * features, features), features)
    chunk_rows = row_count // CHUNKS
    copies = []
    arriving = []
    for chunk in range(CHUNKS):
        for step in range(1, shards):
            piece = pl.ds(chunk * chunk_rows, chunk_rows)
            arriving.append(
                pltpu.make_async_remote_copy(
                    src_ref=tokens.at[piece],
                    dst_ref=rows_out.at[piece, columns],
                    send_sem=token_send.at[step, chunk],
                    recv_sem=token_recv.at[step, chunk],
                    device_id={"tensor": (part + step) % shards},
                )
            )
            arriving[-1].start()
    sends = []
    for step in range(1, chips):
        sends.append(
            pltpu.make_async_remote_copy(
                src_ref=down,
                dst_ref=down_all.at[me],
                send_sem=down_send.at[step],
                recv_sem=down_recv.at[step],
                device_id={"rollout": same_core(step)},
            )
        )
        sends[-1].start()
    copies.append(
        pltpu.make_async_remote_copy(
            src_ref=down,
            dst_ref=down_all.at[me],
            send_sem=forward_send.at[0],
            recv_sem=forward_recv.at[0],
            device_id={"rollout": sibling},
        )
    )
    copies[-1].start()
    for step in range(1, groups):
        copies.append(
            pltpu.make_async_remote_copy(
                src_ref=up,
                dst_ref=up_out.at[me],
                send_sem=up_send.at[step],
                recv_sem=up_recv.at[step],
                device_id={"rollout": (me + step) % groups},
            )
        )
        copies[-1].start()
    own = [
        pltpu.make_async_copy(tokens, rows_out.at[:, columns], local_sem.at[0]),
        pltpu.make_async_copy(down, down_all.at[me], local_sem.at[1]),
        pltpu.make_async_copy(up, up_out.at[me], local_sem.at[2]),
    ]
    for copy in own:
        copy.start()
    for step in range(1, chips):
        sends[step - 1].wait_recv()
        source = same_core(-step)
        copies.append(
            pltpu.make_async_remote_copy(
                src_ref=down_all.at[source],
                dst_ref=down_all.at[source],
                send_sem=forward_send.at[step],
                recv_sem=forward_recv.at[step],
                device_id={"rollout": sibling},
            )
        )
        copies[-1].start()
    for copy in sends:
        copy.wait_send()
    for copy in copies:
        copy.wait()
    for copy in own:
        copy.wait()

    copies = []
    for chunk in range(CHUNKS):
        piece = pl.ds(chunk * chunk_rows, chunk_rows)
        for step in range(1, shards):
            arriving[chunk * (shards - 1) + step - 1].wait_recv()
        total = jnp.zeros((chunk_rows, down.shape[1]), jnp.float32)
        for owner in range(groups):
            block = pl.ds(owner * block_rows, block_rows)
            factor = down_all[inverse[owner]]
            total += jnp.dot(rows_out[piece, block], factor, preferred_element_type=jnp.float32)
        low_out[part, piece] = (adapter_scale * total).astype(low_out.dtype)
        for step in range(1, shards):
            copies.append(
                pltpu.make_async_remote_copy(
                    src_ref=low_out.at[part, piece],
                    dst_ref=low_out.at[part, piece],
                    send_sem=low_send.at[step, chunk],
                    recv_sem=low_recv.at[step, chunk],
                    device_id={"tensor": (part + step) % shards},
                )
            )
            copies[-1].start()
    for copy in arriving:
        copy.wait_send()
    for copy in copies:
        copy.wait()


def gather_all(inverse, tokens, down, up, groups, shards):
    chips = groups // 2
    rows, features = tokens.shape
    dma = pltpu.SemaphoreType.DMA
    vmem = pl.BlockSpec(memory_space=pltpu.VMEM)
    hbm = pl.BlockSpec(memory_space=pl.ANY)
    return pl.pallas_call(
        functools.partial(gather_kernel, groups, shards),
        out_shape=(
            jax.ShapeDtypeStruct((rows, shards * features), tokens.dtype),
            jax.ShapeDtypeStruct((shards, rows, down.shape[1]), jnp.bfloat16),
            jax.ShapeDtypeStruct((groups,) + up.shape, up.dtype),
        ),
        in_specs=[pl.BlockSpec(memory_space=pltpu.SMEM), hbm, vmem, vmem],
        out_specs=[vmem, vmem, vmem],
        scratch_shapes=[
            pltpu.VMEM((groups,) + down.shape, down.dtype),
            dma((3,)),
            dma((shards, CHUNKS)),
            dma((shards, CHUNKS)),
            dma((chips,)),
            dma((chips,)),
            dma((groups,)),
            dma((groups,)),
            dma((chips,)),
            dma((chips,)),
            dma((shards, CHUNKS)),
            dma((shards, CHUNKS)),
        ],
        compiler_params=pltpu.CompilerParams(
            collective_id=0, has_side_effects=True, vmem_limit_bytes=24 * 1024 * 1024
        ),
    )(inverse, tokens, down, up)


def exchange_kernel(groups, outgoing, arrived, local_sem, send_sem, recv_sem):
    me = lax.axis_index("rollout")
    barrier = pltpu.get_barrier_semaphore()
    for step in range(1, groups):
        pl.semaphore_signal(barrier, inc=1, device_id={"rollout": (me + step) % groups})
    pl.semaphore_wait(barrier, groups - 1)
    copies = []
    for step in range(1, groups):
        peer = (me + step) % groups
        copies.append(
            pltpu.make_async_remote_copy(
                src_ref=outgoing.at[peer],
                dst_ref=arrived.at[me],
                send_sem=send_sem.at[step],
                recv_sem=recv_sem.at[step],
                device_id={"rollout": peer},
            )
        )
        copies[-1].start()
    own = pltpu.make_async_copy(outgoing.at[me], arrived.at[me], local_sem)
    own.start()
    for copy in copies:
        copy.wait()
    own.wait()


def exchange(outgoing, groups):
    dma = pltpu.SemaphoreType.DMA
    return pl.pallas_call(
        functools.partial(exchange_kernel, groups),
        out_shape=jax.ShapeDtypeStruct(outgoing.shape, outgoing.dtype),
        in_specs=[pl.BlockSpec(memory_space=pl.ANY)],
        out_specs=pl.BlockSpec(memory_space=pl.ANY),
        scratch_shapes=[dma, dma((groups,)), dma((groups,))],
        compiler_params=pltpu.CompilerParams(collective_id=1, has_side_effects=True),
    )(outgoing)


def body(
    tokens,
    base_key_value_weight,
    key_value_bias,
    adapter_down_blocks,
    adapter_up_blocks,
    owner_shard_lookup,
    lengths,
    routes,
):
    group_count = lax.axis_size("rollout")
    row_count = tokens.shape[0]
    capacity = 2 * row_count // group_count
    width = base_key_value_weight.shape[2]
    order = jnp.arange(group_count, dtype=jnp.int32)
    inverse_permutation = jnp.sum(
        jnp.where(owner_shard_lookup[None, :] == order[:, None], order[None, :], 0), axis=1
    )
    block_rows = adapter_down_blocks.shape[0]
    shards = lax.axis_size("tensor")
    low_width = 2 * adapter_down_blocks.shape[2]
    down_part = lax.dynamic_slice_in_dim(
        adapter_down_blocks.reshape(block_rows, low_width),
        lax.axis_index("tensor") * (low_width // shards),
        low_width // shards,
        axis=1,
    )
    rows, low, up_blocks = gather_all(
        inverse_permutation,
        tokens,
        down_part,
        adapter_up_blocks.reshape(-1, width),
        group_count,
        shards,
    )
    low = low.transpose(1, 0, 2).reshape(row_count, 2, -1)
    up_blocks = up_blocks.reshape((group_count,) + adapter_up_blocks.shape)
    up = up_blocks[inverse_permutation].transpose(1, 0, 2, 3).reshape(2, -1, width)
    update = jnp.einsum("nsr,src->nsc", low, up, preferred_element_type=jnp.float32)
    summed = jnp.einsum(
        "nf,fsc->nsc", rows, base_key_value_weight, preferred_element_type=jnp.float32
    )
    shaped = summed + update + key_value_bias.astype(jnp.float32)[None]
    places = positions_of(lengths[0], row_count)
    keys = rotate(shaped[:, 0], places)
    finished = jnp.concatenate([keys, shaped[:, 1]], axis=1).astype(jnp.bfloat16)
    slot_count = group_count * capacity
    send_slots = slot_index(routes, group_count, capacity)
    selector = (jnp.arange(slot_count, dtype=jnp.int32)[:, None] == send_slots[None, :]).astype(
        jnp.bfloat16
    )
    outgoing = jnp.dot(selector, finished, preferred_element_type=jnp.float32).astype(jnp.bfloat16)
    arrived = exchange(outgoing.reshape(group_count, capacity, 2 * width), group_count)
    return arrived.reshape(slot_count, 2, width)


def solution(mesh):
    in_specs = (
        P("rollout", "tensor"),
        P(None, None, "tensor"),
        P(None, "tensor"),
        P("rollout", None, None),
        P(None, "rollout", "tensor"),
        P(),
        P("rollout", None),
        P("rollout"),
    )
    out_specs = P("rollout", None, "tensor")
    return jax.shard_map(body, mesh=mesh, in_specs=in_specs, out_specs=out_specs, check_vma=False)
```
